32 devices in a mesh: lang: 2 (over y), fsdp: 16 (over z, x, core).
Axes of the slice: x: 2, y: 2, z: 4, core: 2. Of those that a mesh axis runs over, the one named last changes fastest.
Arguments:
- tokens: bfloat16 [2, 768, 8192], P('lang', 'fsdp'), may hold values from -6 to 6
- grad_out: bfloat16 [2, 768, 8192], P('lang', 'fsdp'), may hold values from -24 to 24
- doc_ids: int32 [2, 768], P('lang'), may hold values from 0 to 95, never falling along the last dimension, each value on 1 to 64 neighbouring positions
- w_gate: bfloat16 [8192, 4096], P(None, 'fsdp'), may hold values from -0.0625 to 0.0625
- w_up: bfloat16 [8192, 4096], P(None, 'fsdp'), may hold values from -0.0625 to 0.0625
- w_down: bfloat16 [4096, 8192], P('fsdp'), may hold values from -0.09375 to 0.09375
Outputs:
- grad_tokens: bfloat16 [2, 768, 8192], P('lang', 'fsdp')
- grad_gate: bfloat16 [8192, 4096], P('lang', 'fsdp')
- grad_up: bfloat16 [8192, 4096], P('lang', 'fsdp')
- grad_down: bfloat16 [4096, 8192], P('fsdp', 'lang')
The draws below stay inside these ranges and needn't reach their ends.
Inputs may be any that keep to these rules, and one draw needn't show every extreme that they name: `doc_ids`: document numbers never fall along a group's pack.
All inputs are finite; a program needn't handle non-finite values.
Results may differ from the reference program's by a relative error of at most 0.015.
Values may be sent and summed in bfloat16 or wider, within the bound.
A program may use at most 192 MiB of HBM per device.

```python
import math
import jax
import jax.numpy as jnp
import numpy as np
from jax import lax

D = 8192
HID_DEV = 256
LANGS = 2
HS = 4096
TL = 768
DOCS = 96
DOC_MOST = 64
N_FSDP = 16


def draw_grad_out(key, part):
    ladder = jnp.arange(LANGS, dtype=jnp.float32) / max(LANGS - 1, 1)
    scales = jnp.exp(ladder * jnp.log(3.0))
    values = jax.random.normal(key, (LANGS, TL, D), jnp.float32)
    values = jnp.clip(values * scales[:, None, None], -24.0, 24.0)
    return values.astype(jnp.bfloat16)


def block_scale(own_key, extent, pieces, low, largest):
    loudness = 1.0
    for position, shards_of in pieces:
        draws = jax.random.uniform(jax.random.fold_in(jax.random.fold_in(own_key, 6), position), (shards_of,), jnp.float32, low / len(pieces), largest / len(pieces))
        loudness = loudness * jnp.repeat(jnp.exp(draws), extent[position] // shards_of).reshape((-1,) + (1,) * (len(extent) - 1 - position))
    return loudness


def profile(count, total, reach, lean):
    portions = [(1 << 20) // math.isqrt(rank ** lean) + 1 for rank in range(2, count + 1)]
    rest, given = total - reach - (count - 1), [1] * (count - 1)
    while rest > 0:
        movable = [i for i in range(count - 1) if given[i] < reach]
        mass, left = sum([portions[i] for i in movable]), rest
        for i in movable:
            addition = min(reach - given[i], max(1, left * portions[i] // mass), rest)
            given[i] = given[i] + addition
            rest = rest - addition
    return np.array([reach] + given)


def ragged(stream_key, number_of, total, limit, skew):
    if number_of == 2:
        one = jax.random.randint(stream_key, (), max(1, total - limit), min(limit, total - 1) + 1)
        return jnp.stack([one, total - one])
    sizes = jnp.asarray(profile(number_of, total, limit, skew), jnp.int32)
    twos = (number_of - 1) // 2
    source_of, sink = sizes[1:1 + 2 * twos:2], sizes[2:2 + 2 * twos:2]
    slack = jnp.minimum(source_of - 1, limit - sink)
    shifted = jax.random.randint(jax.random.fold_in(stream_key, 1), (twos,), 0, 1 << 20) % (slack + 1)
    sizes = sizes.at[1:1 + 2 * twos:2].set(source_of - shifted).at[2:2 + 2 * twos:2].set(sink + shifted)
    return sizes[jax.random.permutation(jax.random.fold_in(stream_key, 2), number_of)]


def noise(key, dims, scale, limit, shards=(), kind=jnp.bfloat16):
    result = jax.random.normal(key, dims, jnp.float32) * scale
    if len(shards) > 0:
        result = block_scale(key, dims, shards, -0.22, 0.18) * result
    return jnp.clip(result, min=-limit, max=limit).astype(kind)


def setup_inputs(seed: int = 0) -> dict:
    seeds = jax.random.split(jax.random.key(seed), 7)
    tokens = noise(seeds[0], (LANGS, TL, D), 1.0, 6.0, ((0, 2), (1, 16)))
    grad_out = draw_grad_out(jax.random.fold_in(seeds[6], 71), 0)
    doc_ids = jax.vmap(lambda own: jnp.searchsorted(jnp.cumsum(ragged(own, DOCS, TL, DOC_MOST, 2)), jnp.arange(TL), side="right"))(jax.random.split(seeds[2], LANGS)).reshape((LANGS, TL)).astype(jnp.int32)
    w_gate = noise(seeds[3], (D, HS), D ** -0.5, 0.0625, ((1, 16),))
    w_up = noise(seeds[4], (D, HS), D ** -0.5, 0.0625, ((1, 16),))
    w_down = noise(seeds[5], (HS, D), HS ** -0.5, 0.09375, ((0, 16),))
    return {"tokens": tokens, "grad_out": grad_out, "doc_ids": doc_ids, "w_gate": w_gate, "w_up": w_up, "w_down": w_down}


epsilon = 1e-6


def contract_rows(left, right):
    return lax.dot_general(left, right, (((0,), (0,)), ((), ())), preferred_element_type=jnp.float32)


def contract_cols(left, right):
    return lax.dot_general(left, right, (((1,), (1,)), ((), ())), preferred_element_type=jnp.float32)


def forward_parts(features, upstream, segment, w_gate, w_up, w_down):
    counts = jnp.sum((segment[:, None] == segment[None, :]).astype(jnp.float32), axis=1)
    inverse = 1.0 / counts
    gate_pre = jnp.dot(features, w_gate, preferred_element_type=jnp.float32)
    up_pre = jnp.dot(features, w_up, preferred_element_type=jnp.float32)
    gate_sig = jax.nn.sigmoid(gate_pre)
    activated = gate_pre * gate_sig
    hidden = (activated * up_pre * inverse[:, None]).astype(jnp.bfloat16)
    hid_grad = contract_cols(upstream, w_down) * inverse[:, None]
    gate_grad = (hid_grad * up_pre * gate_sig * (1.0 + gate_pre * (1.0 - gate_sig))).astype(jnp.bfloat16)
    up_grad = (hid_grad * activated).astype(jnp.bfloat16)
    return hidden, gate_grad, up_grad


def reference(tokens, grad_out, doc_ids, w_gate, w_up, w_down):
    input_grads = []
    saved = []
    ratio_list = []
    for language in range(LANGS):
        features = tokens[language]
        upstream = grad_out[language]
        hidden, gate_grad, up_grad = forward_parts(features, upstream, doc_ids[language], w_gate, w_up, w_down)
        summed = jnp.zeros((TL, D), jnp.float32)
        for column_block in range(N_FSDP):
            lower = column_block * HID_DEV
            upper = lower + HID_DEV
            partial_sum = contract_cols(gate_grad[:, lower:upper], w_gate[:, lower:upper])
            partial_sum = partial_sum + contract_cols(up_grad[:, lower:upper], w_up[:, lower:upper])
            rounded = lax.optimization_barrier(partial_sum.astype(jnp.bfloat16))
            summed = summed + rounded.astype(jnp.float32)
        input_grads.append(summed.astype(jnp.bfloat16))
        g_gate = contract_rows(features, gate_grad)
        g_up = contract_rows(features, up_grad)
        g_down = contract_rows(upstream, hidden)
        moment = (jnp.sum(g_gate * g_gate, axis=0) + jnp.sum(g_up * g_up, axis=0) + jnp.sum(g_down * g_down, axis=0)) / (3.0 * D) + epsilon
        ratio_list.append(1.0 / moment)
        saved.append((hidden, gate_grad, up_grad))
    ratios = jnp.stack(ratio_list)
    summed_ratio = jnp.sum(ratios, axis=0)
    acc_gate = jnp.zeros((D, HS), jnp.float32)
    acc_up = jnp.zeros((D, HS), jnp.float32)
    acc_down = jnp.zeros((D, HS), jnp.float32)
    for language in range(LANGS):
        hidden, gate_grad, up_grad = saved[language]
        weight_row = (ratios[language] / summed_ratio)[None, :]
        term_gate = lax.optimization_barrier((contract_rows(tokens[language], gate_grad) * weight_row).astype(jnp.bfloat16))
        term_up = lax.optimization_barrier((contract_rows(tokens[language], up_grad) * weight_row).astype(jnp.bfloat16))
        term_down = lax.optimization_barrier((contract_rows(grad_out[language], hidden) * weight_row).astype(jnp.bfloat16))
        acc_gate = acc_gate + term_gate.astype(jnp.float32)
        acc_up = acc_up + term_up.astype(jnp.float32)
        acc_down = acc_down + term_down.astype(jnp.float32)
    grad_tokens = jnp.stack(input_grads)
    return grad_tokens, acc_gate.astype(jnp.bfloat16), acc_up.astype(jnp.bfloat16), acc_down.T.astype(jnp.bfloat16)
```

```python
import functools

import jax
import jax.numpy as jnp
from jax import lax
from jax.experimental import pallas as pl
from jax.experimental.pallas import tpu as pltpu
from jax.sharding import PartitionSpec as P

epsilon = 1e-06
CORES = 2


def contract_rows(left, right):
    return lax.dot_general(
        left, right, (((0,), (0,)), ((), ())), preferred_element_type=jnp.float32
    )


def contract_cols(left, right):
    return lax.dot_general(
        left, right, (((1,), (1,)), ((), ())), preferred_element_type=jnp.float32
    )


def chip_of(position, chips):
    back = position // (chips // 2)
    return (1 - back) * 2 * position + back * (2 * (chips - 1 - position) + 1)


def position_of(chip, chips):
    odd = chip % 2
    return (1 - odd) * (chip // 2) + odd * (chips - 1 - chip // 2)


def gather_kernel(
    langs, shards, tok_ref, up_ref, tok_out, up_out,
    ring_send, ring_recv, sib_send, sib_recv, lang_send, lang_recv, local_sem,
):
    chips = shards // CORES
    rows = tok_ref.shape[0]
    width = tok_ref.shape[1] // langs
    lang = lax.axis_index("lang")
    me = lax.axis_index("fsdp")
    core = me % CORES
    place = position_of(me // CORES, chips)
    right = chip_of((place + 1) % chips, chips) * CORES + core
    left = chip_of((place + chips - 1) % chips, chips) * CORES + core
    sibling = me + 1 - 2 * core

    barrier = pltpu.get_barrier_semaphore()
    peers = [(lang, right), (lang, left), (lang, sibling)]
    peers += [((lang + d) % langs, me) for d in range(1, langs)]
    for peer in peers:
        pl.semaphore_signal(barrier, inc=1, device_id=peer, device_id_type=pl.DeviceIdType.MESH)
    pl.semaphore_wait(barrier, len(peers))

    ins = (tok_ref, up_ref)
    outs = (tok_out, up_out)
    nexts = (right, left)

    def block(array, group, shard):
        return outs[array].at[group, pl.ds(pl.multiple_of(shard * rows, rows), rows), :]

    def own(array, group):
        return ins[array].at[:, pl.ds(pl.multiple_of(group * width, width), width)]

    def remote(src, dst, send, recv, device):
        return pltpu.make_async_remote_copy(
            src_ref=src, dst_ref=dst, send_sem=send, recv_sem=recv,
            device_id=device, device_id_type=pl.DeviceIdType.MESH,
        )

    def origin(array, step):
        shift = chips - step if array == 0 else step
        return chip_of((place + shift) % chips, chips) * CORES + core

    sends = []
    locals_ = []
    lang_copies = {}
    for array in range(2):
        for d in range(1, langs):
            peer = (lang + d) % langs
            copy = remote(
                own(array, peer), block(array, lang, me),
                lang_send.at[array, d], lang_recv.at[array, d], (peer, me),
            )
            copy.start()
            lang_copies[array, d] = copy
    for array in range(2):
        copy = pltpu.make_async_copy(own(array, lang), block(array, lang, me), local_sem.at[array])
        copy.start()
        locals_.append(copy)

    ring = {}
    sib = {}

    def forward(array, d, step, src):
        group = (lang + langs - d) % langs
        shard = origin(array, step)
        dst = block(array, group, shard)
        if step < chips - 1:
            copy = remote(
                src, dst, ring_send.at[array, d, step], ring_recv.at[array, d, step],
                (lang, nexts[array]),
            )
            copy.start()
            ring[array, d, step] = copy
        copy = remote(
            src, dst, sib_send.at[array, d, step], sib_recv.at[array, d, step], (lang, sibling)
        )
        copy.start()
        sib[array, d, step] = copy

    for step in range(chips):
        for d in range(langs):
            for array in range(2):
                group = (lang + langs - d) % langs
                if step == 0:
                    if d == 0:
                        src = own(array, lang)
                    else:
                        lang_copies[array, d].wait_recv()
                        src = block(array, group, me)
                else:
                    ring[array, d, step - 1].wait_recv()
                    src = block(array, group, origin(array, step))
                forward(array, d, step, src)
    for copy in locals_:
        copy.wait()
    for copy in lang_copies.values():
        copy.wait_send()
    for copy in ring.values():
        copy.wait_send()
    for copy in sib.values():
        copy.wait()


def gather(tokens, grad_out, langs, shards):
    rows, width = tokens.shape
    chips = shards // CORES
    out = jax.ShapeDtypeStruct((langs, rows * shards, width // langs), tokens.dtype)
    dma = pltpu.SemaphoreType.DMA
    return pl.pallas_call(
        functools.partial(gather_kernel, langs, shards),
        out_shape=(out, out),
        in_specs=[pl.BlockSpec(memory_space=pl.ANY)] * 2,
        out_specs=(pl.BlockSpec(memory_space=pl.ANY),) * 2,
        scratch_shapes=[
            dma((2, langs, chips)), dma((2, langs, chips)),
            dma((2, langs, chips)), dma((2, langs, chips)),
            dma((2, langs)), dma((2, langs)), dma((2,)),
        ],
        compiler_params=pltpu.CompilerParams(collective_id=0, has_side_effects=True),
        name="gather",
    )(tokens, grad_out)


def scatter_kernel(
    langs, shards, part_ref, out_ref, mine, sib_in, ring_in,
    load_sem, sib_send, sib_recv, ring_send, ring_recv, lang_send, lang_recv, local_sem,
):
    chips = shards // CORES
    rows, width = mine.shape[2:]
    lang = lax.axis_index("lang")
    me = lax.axis_index("fsdp")
    core = me % CORES
    place = position_of(me // CORES, chips)
    right = chip_of((place + 1) % chips, chips) * CORES + core
    left = chip_of((place + chips - 1) % chips, chips) * CORES + core
    sibling = me + 1 - 2 * core

    barrier = pltpu.get_barrier_semaphore()
    peers = [(lang, right), (lang, left), (lang, sibling)]
    peers += [((lang + d) % langs, me) for d in range(1, langs)]
    for peer in peers:
        pl.semaphore_signal(barrier, inc=1, device_id=peer, device_id_type=pl.DeviceIdType.MESH)
    pl.semaphore_wait(barrier, len(peers))

    def remote(src, dst, send, recv, device):
        return pltpu.make_async_remote_copy(
            src_ref=src, dst_ref=dst, send_sem=send, recv_sem=recv,
            device_id=device, device_id_type=pl.DeviceIdType.MESH,
        )

    def piece(d, step, own):
        shift = step + 1 if d % 2 else chips - 1 - step
        chip = chip_of((place + shift) % chips, chips)
        shard = chip * CORES + (core if own else 1 - core)
        start = ((lang + d) % langs) * (shards * rows) + shard * rows
        return part_ref.at[pl.ds(pl.multiple_of(start, rows), rows), :]

    loads, sib, ring = {}, {}, {}
    order = [(step, d) for step in range(chips) for d in range(langs)]
    for step, d in order:
        sib[d, step] = remote(
            piece(d, step, False), sib_in.at[d, step],
            sib_send.at[d, step], sib_recv.at[d, step], (lang, sibling),
        )
        sib[d, step].start()
        loads[d, step] = pltpu.make_async_copy(
            piece(d, step, True), mine.at[d, step], load_sem.at[d, step]
        )
        loads[d, step].start()
    tail = []
    for step, d in order:
        loads[d, step].wait()
        sib[d, step].wait_recv()
        total = mine[d, step].astype(jnp.float32) + sib_in[d, step].astype(jnp.float32)
        if step:
            ring[d, step - 1].wait_recv()
            total = total + ring_in[d, step - 1].astype(jnp.float32)
        mine[d, step] = total.astype(mine.dtype)
        if step < chips - 1:
            ring[d, step] = remote(
                mine.at[d, step], ring_in.at[d, step],
                ring_send.at[d, step], ring_recv.at[d, step],
                (lang, left if d % 2 else right),
            )
            ring[d, step].start()
        else:
            dst = out_ref.at[:, pl.ds(pl.multiple_of(lang * width, width), width)]
            if d == 0:
                copy = pltpu.make_async_copy(mine.at[d, step], dst, local_sem)
            else:
                copy = remote(
                    mine.at[d, step], dst, lang_send.at[d], lang_recv.at[d],
                    ((lang + d) % langs, me),
                )
            copy.start()
            tail.append(copy)
    for copy in tail:
        copy.wait()
    for copy in list(sib.values()) + list(ring.values()):
        copy.wait_send()


def scatter(partial, langs, shards):
    width = partial.shape[1]
    rows = partial.shape[0] // (langs * shards)
    chips = shards // CORES
    dma = pltpu.SemaphoreType.DMA
    return pl.pallas_call(
        functools.partial(scatter_kernel, langs, shards),
        out_shape=jax.ShapeDtypeStruct((rows, width * langs), partial.dtype),
        in_specs=[pl.BlockSpec(memory_space=pl.ANY)],
        out_specs=pl.BlockSpec(memory_space=pl.ANY),
        scratch_shapes=[
            pltpu.VMEM((langs, chips, rows, width), partial.dtype),
            pltpu.VMEM((langs, chips, rows, width), partial.dtype),
            pltpu.VMEM((langs, chips, rows, width), partial.dtype),
            dma((langs, chips)), dma((langs, chips)), dma((langs, chips)),
            dma((langs, chips)), dma((langs, chips)), dma((langs,)), dma((langs,)), dma,
        ],
        compiler_params=pltpu.CompilerParams(
            collective_id=1, has_side_effects=True, vmem_limit_bytes=40 * 2**20
        ),
        name="scatter",
    )(partial)


def swap_sum(value, langs):
    sent = value.astype(jnp.bfloat16)
    total = value
    for d in range(1, langs):
        got = lax.ppermute(sent, "lang", [(i, (i + d) % langs) for i in range(langs)])
        total = total + got.astype(jnp.float32)
    return total


def body(langs, shards, tokens, grad_out, doc_ids, w_gate, w_up, w_down):
    lang = lax.axis_index("lang")
    depth = w_gate.shape[0]
    width = depth // langs
    feats, ups = gather(tokens[0], grad_out[0], langs, shards)
    count_tokens = feats.shape[1]
    feats = feats.reshape(langs * count_tokens, width)
    ups = ups.reshape(langs * count_tokens, width)
    segment = doc_ids[0]
    counts = jnp.sum((segment[:, None] == segment[None, :]).astype(jnp.float32), axis=1)
    inverse = lax.all_gather(1.0 / counts, "lang", axis=0, tiled=True)[:, None]
    wg = lax.dynamic_slice_in_dim(w_gate, lang * width, width, 0)
    wu = lax.dynamic_slice_in_dim(w_up, lang * width, width, 0)
    wd = lax.dynamic_slice_in_dim(w_down, lang * width, width, 1)
    gate_pre = swap_sum(jnp.dot(feats, wg, preferred_element_type=jnp.float32), langs)
    up_pre = swap_sum(jnp.dot(feats, wu, preferred_element_type=jnp.float32), langs)
    hid_grad = swap_sum(contract_cols(ups, wd), langs) * inverse
    gate_sig = jax.nn.sigmoid(gate_pre)
    activated = gate_pre * gate_sig
    hidden = (activated * up_pre * inverse).astype(jnp.bfloat16)
    gate_grad = (hid_grad * up_pre * gate_sig * (1.0 + gate_pre * (1.0 - gate_sig))).astype(
        jnp.bfloat16
    )
    up_grad = (hid_grad * activated).astype(jnp.bfloat16)

    partial = contract_cols(
        jnp.concatenate([gate_grad, up_grad], axis=1), jnp.concatenate([wg, wu], axis=1)
    ).astype(jnp.bfloat16)
    grad_tokens = scatter(partial, langs, shards)[None]

    def by_lang(left, right):
        left = left.reshape(langs, count_tokens, -1)
        right = right.reshape(langs, count_tokens, -1)
        return [contract_rows(left[l], right[l]) for l in range(langs)]

    g_gate = by_lang(feats, gate_grad)
    g_up = by_lang(feats, up_grad)
    g_down = by_lang(hidden, ups)
    squares = jnp.stack([
        jnp.sum(g_gate[l] ** 2, axis=0) + jnp.sum(g_up[l] ** 2, axis=0) + jnp.sum(g_down[l] ** 2, axis=1)
        for l in range(langs)
    ])
    moment = lax.psum(squares, "lang") / (3.0 * depth) + epsilon
    ratios = 1.0 / moment
    share = ratios / jnp.sum(ratios, axis=0, keepdims=True)

    def weigh(parts, axis):
        total = 0.0
        for l in range(langs):
            total = total + parts[l] * (share[l][None, :] if axis else share[l][:, None])
        return total.astype(jnp.bfloat16)

    return grad_tokens, weigh(g_gate, 1), weigh(g_up, 1), weigh(g_down, 0)


def solution(mesh):
    return jax.shard_map(
        functools.partial(body, mesh.shape["lang"], mesh.shape["fsdp"]),
        mesh=mesh,
        in_specs=(
            P("lang", "fsdp", None),
            P("lang", "fsdp", None),
            P("lang", None),
            P(None, "fsdp"),
            P(None, "fsdp"),
            P("fsdp", None),
        ),
        out_specs=(
            P("lang", "fsdp", None),
            P("lang", "fsdp"),
            P("lang", "fsdp"),
            P("fsdp", "lang"),
        ),
        check_vma=False,
    )
```

```python
import functools

import jax
import jax.numpy as jnp
from jax import lax
from jax.experimental import pallas as pl
from jax.experimental.pallas import tpu as pltpu
from jax.sharding import PartitionSpec as P

epsilon = 1e-06
CORES = 2
VMEM_ARRIVALS = 8 * 2**20


def contract_rows(left, right):
    return lax.dot_general(
        left, right, (((0,), (0,)), ((), ())), preferred_element_type=jnp.float32
    )


def contract_cols(left, right):
    return lax.dot_general(
        left, right, (((1,), (1,)), ((), ())), preferred_element_type=jnp.float32
    )


def chip_of(position, chips):
    back = position // (chips // 2)
    return (1 - back) * 2 * position + back * (2 * (chips - 1 - position) + 1)


def position_of(chip, chips):
    odd = chip % 2
    return (1 - odd) * (chip // 2) + odd * (chips - 1 - chip // 2)


def gather_kernel(
    langs, shards, swaps, tok_ref, up_ref, wg_ref, wu_ref, wd_ref, inv_ref,
    tok_out, up_out, pre_out, back_out, inv_out,
    weights, down, feats, ups, pre_send, back_send, pre_recv, back_recv,
    ring_send, ring_recv, sib_send, sib_recv, lang_send, lang_recv, local_sem,
    weight_sem, part_send, part_recv, inv_send, inv_recv,
):
    chips = shards // CORES
    rows = tok_ref.shape[0]
    width = tok_ref.shape[1] // langs
    units = wg_ref.shape[1]
    lang = lax.axis_index("lang")
    me = lax.axis_index("fsdp")
    core = me % CORES
    place = position_of(me // CORES, chips)
    right = chip_of((place + 1) % chips, chips) * CORES + core
    left = chip_of((place + chips - 1) % chips, chips) * CORES + core
    sibling = me + 1 - 2 * core

    barrier = pltpu.get_barrier_semaphore()
    peers = [(lang, right), (lang, left), (lang, sibling)]
    peers += [((lang + d) % langs, me) for d in range(1, langs)]
    for peer in peers:
        pl.semaphore_signal(barrier, inc=1, device_id=peer, device_id_type=pl.DeviceIdType.MESH)
    pl.semaphore_wait(barrier, len(peers))

    ins = (tok_ref, up_ref)
    outs = (tok_out, up_out)
    nexts = (right, left)
    sents = (pre_send, back_send)
    recvs = (pre_recv, back_recv)
    sums = (pre_out, back_out)

    def block(array, group, shard):
        return outs[array].at[group, pl.ds(pl.multiple_of(shard * rows, rows), rows), :]

    def own(array, group):
        return ins[array].at[:, pl.ds(pl.multiple_of(group * width, width), width)]

    def remote(src, dst, send, recv, device):
        return pltpu.make_async_remote_copy(
            src_ref=src, dst_ref=dst, send_sem=send, recv_sem=recv,
            device_id=device, device_id_type=pl.DeviceIdType.MESH,
        )

    def chip_at(array, step):
        shift = step if array else chips - step
        return chip_of((place + shift) % chips, chips)

    def group_at(d):
        return (lang + langs - d) % langs

    def ring_copy(array, d, step):
        held = block(array, group_at(d), chip_at(array, step) * CORES + core)
        return remote(
            held, held, ring_send.at[array, d, step], ring_recv.at[array, d, step],
            (lang, nexts[array]),
        )

    def sib_copy(array, d, step):
        held = block(array, group_at(d), chip_at(array, step) * CORES + core)
        return remote(
            held, held, sib_send.at[array, d, step], sib_recv.at[array, d, step], (lang, sibling)
        )

    def part_copy(array, e, d, step):
        group, chip = group_at(d), chip_at(array, step)
        return remote(
            sents[array].at[group, chip], recvs[array].at[e - 1, group, chip],
            part_send.at[array, e, group, chip], part_recv.at[array, e, group, chip],
            ((lang + e) % langs, me),
        )

    lang_copies, first, inv_copies = {}, [], []
    for array in range(2):
        for d in range(1, langs):
            peer = (lang + d) % langs
            copy = remote(
                own(array, peer), block(array, lang, me),
                lang_send.at[array, d], lang_recv.at[array, d], (peer, me),
            )
            copy.start()
            lang_copies[array, d] = copy
        copy = pltpu.make_async_copy(own(array, lang), block(array, lang, me), local_sem.at[array, 0])
        copy.start()
        first.append(copy)
    for d in range(1, langs):
        copy = remote(
            inv_ref, inv_out.at[lang], inv_send.at[d], inv_recv.at[d], ((lang + d) % langs, me)
        )
        copy.start()
        inv_copies.append(copy)
    inv_out[lang] = inv_ref[...]
    slab = pl.ds(pl.multiple_of(lang * width, width), width)
    loads = [
        pltpu.make_async_copy(wg_ref.at[slab, :], weights.at[:, pl.ds(0, units)], weight_sem.at[0]),
        pltpu.make_async_copy(
            wu_ref.at[slab, :], weights.at[:, pl.ds(units, units)], weight_sem.at[1]
        ),
        pltpu.make_async_copy(wd_ref.at[:, slab], down, weight_sem.at[2]),
    ]

    for d in range(langs):
        for array in range(2):
            if d == 0:
                first[array].wait()
            else:
                lang_copies[array, d].wait_recv()
            ring_copy(array, d, 0).start()
            sib_copy(array, d, 0).start()
    for copy in loads:
        copy.start()
    for copy in loads:
        copy.wait()

    def compute(step, d):
        group = group_at(d)
        fetches = []
        for array in range(2):
            sib_copy(array, d, step).wait_recv()
            chip = chip_at(array, step)
            pair = pl.ds(pl.multiple_of(chip * (CORES * rows), CORES * rows), CORES * rows)
            copy = pltpu.make_async_copy(
                outs[array].at[group, pair, :], (feats, ups)[array], local_sem.at[array, 1]
            )
            copy.start()
            fetches.append(copy)
        for array in range(2):
            fetches[array].wait()
            chip = chip_at(array, step)
            if array == 0:
                value = jnp.dot(feats[...], weights[...], preferred_element_type=jnp.float32)
            else:
                value = contract_cols(ups[...], down[...])
            sums[array][group, chip] = value
            if swaps:
                sents[array][group, chip] = value.astype(jnp.bfloat16)
            for e in range(1, swaps + 1):
                part_copy(array, e, d, step).start()

    def advance(step, carry):
        for d in range(langs):
            for array in range(2):
                ring_copy(array, d, step - 1).wait_recv()

                @pl.when(step < chips - 1)
                def _():
                    ring_copy(array, d, step).start()

                sib_copy(array, d, step).start()
            compute(step - 1, d)
        return carry

    lax.fori_loop(1, chips, advance, 0)
    for d in range(langs):
        compute(chips - 1, d)

    def finish(step, carry):
        for d in range(langs):
            for array in range(2):
                group, chip = group_at(d), chip_at(array, step)
                for e in range(1, swaps + 1):
                    part_copy(array, e, d, step).wait()
                    sums[array][group, chip] += recvs[array][e - 1, group, chip].astype(jnp.float32)
                sib_copy(array, d, step).wait_send()

                @pl.when(step < chips - 1)
                def _():
                    ring_copy(array, d, step).wait_send()
        return carry

    lax.fori_loop(0, chips, finish, 0)
    for copy in lang_copies.values():
        copy.wait_send()
    for copy in inv_copies:
        copy.wait()


def gather(tokens, grad_out, w_gate, w_up, w_down, inverse, langs, shards, swaps):
    rows, depth = tokens.shape
    width = depth // langs
    units = w_gate.shape[1]
    chips = shards // CORES
    pair = CORES * rows
    held = (langs, chips, pair) if swaps else (1, 1, pair)
    out = jax.ShapeDtypeStruct((langs, rows * shards, width), tokens.dtype)
    dma = pltpu.SemaphoreType.DMA
    any_space = pl.BlockSpec(memory_space=pl.ANY)
    vmem = pl.BlockSpec(memory_space=pltpu.VMEM)
    return pl.pallas_call(
        functools.partial(gather_kernel, langs, shards, swaps),
        out_shape=(
            out, out,
            jax.ShapeDtypeStruct((langs, chips, pair, 2 * units), jnp.float32),
            jax.ShapeDtypeStruct((langs, chips, pair, units), jnp.float32),
            jax.ShapeDtypeStruct((langs,) + inverse.shape, jnp.float32),
        ),
        in_specs=[any_space] * 5 + [vmem],
        out_specs=(any_space, any_space, vmem, vmem, vmem),
        scratch_shapes=[
            pltpu.VMEM((width, 2 * units), w_gate.dtype),
            pltpu.VMEM((units, width), w_down.dtype),
            pltpu.VMEM((pair, width), tokens.dtype),
            pltpu.VMEM((pair, width), tokens.dtype),
            pltpu.VMEM(held + (2 * units,), jnp.bfloat16),
            pltpu.VMEM(held + (units,), jnp.bfloat16),
            pltpu.VMEM((max(swaps, 1),) + held + (2 * units,), jnp.bfloat16),
            pltpu.VMEM((max(swaps, 1),) + held + (units,), jnp.bfloat16),
            dma((2, langs, chips)), dma((2, langs, chips)),
            dma((2, langs, chips)), dma((2, langs, chips)),
            dma((2, langs)), dma((2, langs)), dma((2, 2)), dma((3,)),
            dma((2, langs, langs, chips)), dma((2, langs, langs, chips)),
            dma((langs,)), dma((langs,)),
        ],
        compiler_params=pltpu.CompilerParams(
            collective_id=0, has_side_effects=True, vmem_limit_bytes=48 * 2**20
        ),
        name="gather",
    )(tokens, grad_out, w_gate, w_up, w_down, inverse)


def scatter_kernel(
    langs, shards, part_ref, out_ref, mine, sib_in, ring_in,
    load_sem, sib_send, sib_recv, ring_send, ring_recv, lang_send, lang_recv, local_sem,
):
    chips = shards // CORES
    rows, width = mine.shape[2:]
    lang = lax.axis_index("lang")
    me = lax.axis_index("fsdp")
    core = me % CORES
    place = position_of(me // CORES, chips)
    right = chip_of((place + 1) % chips, chips) * CORES + core
    left = chip_of((place + chips - 1) % chips, chips) * CORES + core
    sibling = me + 1 - 2 * core

    barrier = pltpu.get_barrier_semaphore()
    peers = [(lang, right), (lang, left), (lang, sibling)]
    peers += [((lang + d) % langs, me) for d in range(1, langs)]
    for peer in peers:
        pl.semaphore_signal(barrier, inc=1, device_id=peer, device_id_type=pl.DeviceIdType.MESH)
    pl.semaphore_wait(barrier, len(peers))

    def remote(src, dst, send, recv, device):
        return pltpu.make_async_remote_copy(
            src_ref=src, dst_ref=dst, send_sem=send, recv_sem=recv,
            device_id=device, device_id_type=pl.DeviceIdType.MESH,
        )

    def piece(d, step, own):
        shift = step + 1 if d % 2 else chips - 1 - step
        chip = chip_of((place + shift) % chips, chips)
        shard = chip * CORES + (core if own else 1 - core)
        start = ((lang + d) % langs) * (shards * rows) + shard * rows
        return part_ref.at[pl.ds(pl.multiple_of(start, rows), rows), :]

    loads, sib, ring = {}, {}, {}
    order = [(step, d) for step in range(chips) for d in range(langs)]
    for step, d in order:
        sib[d, step] = remote(
            piece(d, step, False), sib_in.at[d, step],
            sib_send.at[d, step], sib_recv.at[d, step], (lang, sibling),
        )
        sib[d, step].start()
        loads[d, step] = pltpu.make_async_copy(
            piece(d, step, True), mine.at[d, step], load_sem.at[d, step]
        )
        loads[d, step].start()
    tail = []
    for step, d in order:
        loads[d, step].wait()
        sib[d, step].wait_recv()
        total = mine[d, step].astype(jnp.float32) + sib_in[d, step].astype(jnp.float32)
        if step:
            ring[d, step - 1].wait_recv()
            total = total + ring_in[d, step - 1].astype(jnp.float32)
        mine[d, step] = total.astype(mine.dtype)
        if step < chips - 1:
            ring[d, step] = remote(
                mine.at[d, step], ring_in.at[d, step],
                ring_send.at[d, step], ring_recv.at[d, step],
                (lang, left if d % 2 else right),
            )
            ring[d, step].start()
        else:
            dst = out_ref.at[:, pl.ds(pl.multiple_of(lang * width, width), width)]
            if d == 0:
                copy = pltpu.make_async_copy(mine.at[d, step], dst, local_sem)
            else:
                copy = remote(
                    mine.at[d, step], dst, lang_send.at[d], lang_recv.at[d],
                    ((lang + d) % langs, me),
                )
            copy.start()
            tail.append(copy)
    for copy in tail:
        copy.wait()
    for copy in list(sib.values()) + list(ring.values()):
        copy.wait_send()


def scatter(partial, langs, shards):
    width = partial.shape[1]
    rows = partial.shape[0] // (langs * shards)
    chips = shards // CORES
    dma = pltpu.SemaphoreType.DMA
    return pl.pallas_call(
        functools.partial(scatter_kernel, langs, shards),
        out_shape=jax.ShapeDtypeStruct((rows, width * langs), partial.dtype),
        in_specs=[pl.BlockSpec(memory_space=pl.ANY)],
        out_specs=pl.BlockSpec(memory_space=pl.ANY),
        scratch_shapes=[
            pltpu.VMEM((langs, chips, rows, width), partial.dtype),
            pltpu.VMEM((langs, chips, rows, width), partial.dtype),
            pltpu.VMEM((langs, chips, rows, width), partial.dtype),
            dma((langs, chips)), dma((langs, chips)), dma((langs, chips)),
            dma((langs, chips)), dma((langs, chips)), dma((langs,)), dma((langs,)), dma,
        ],
        compiler_params=pltpu.CompilerParams(
            collective_id=1, has_side_effects=True, vmem_limit_bytes=40 * 2**20
        ),
        name="scatter",
    )(partial)


def swap_sum(value, langs):
    sent = value.astype(jnp.bfloat16)
    total = value
    for d in range(1, langs):
        got = lax.ppermute(sent, "lang", [(i, (i + d) % langs) for i in range(langs)])
        total = total + got.astype(jnp.float32)
    return total


def body(langs, shards, tokens, grad_out, doc_ids, w_gate, w_up, w_down):
    lang = lax.axis_index("lang")
    depth = w_gate.shape[0]
    width = depth // langs
    segment = doc_ids[0]
    counts = jnp.sum((segment[:, None] == segment[None, :]).astype(jnp.float32), axis=1)
    units = w_gate.shape[1]
    arrives = (langs - 1) * langs * tokens.shape[1] * shards * 3 * units * 2
    swaps = langs - 1 if arrives <= VMEM_ARRIVALS else 0
    feats, ups, pre, back, inverse = gather(
        tokens[0], grad_out[0], w_gate, w_up, w_down, (1.0 / counts)[None], langs, shards, swaps
    )
    if not swaps:
        pre, back = swap_sum(pre, langs), swap_sum(back, langs)
    count_tokens = feats.shape[1]
    feats = feats.reshape(langs * count_tokens, width)
    ups = ups.reshape(langs * count_tokens, width)
    inverse = inverse.reshape(-1)[:, None]
    wg = lax.dynamic_slice_in_dim(w_gate, lang * width, width, 0)
    wu = lax.dynamic_slice_in_dim(w_up, lang * width, width, 0)
    pre = pre.reshape(-1, 2 * units)
    gate_pre, up_pre = pre[:, :units], pre[:, units:]
    hid_grad = back.reshape(-1, units) * inverse
    gate_sig = jax.nn.sigmoid(gate_pre)
    activated = gate_pre * gate_sig
    hidden = (activated * up_pre * inverse).astype(jnp.bfloat16)
    gate_grad = (hid_grad * up_pre * gate_sig * (1.0 + gate_pre * (1.0 - gate_sig))).astype(
        jnp.bfloat16
    )
    up_grad = (hid_grad * activated).astype(jnp.bfloat16)

    partial = contract_cols(
        jnp.concatenate([gate_grad, up_grad], axis=1), jnp.concatenate([wg, wu], axis=1)
    ).astype(jnp.bfloat16)
    grad_tokens = scatter(partial, langs, shards)[None]

    def by_lang(left, right):
        left = left.reshape(langs, count_tokens, -1)
        right = right.reshape(langs, count_tokens, -1)
        return [contract_rows(left[l], right[l]) for l in range(langs)]

    g_gate = by_lang(feats, gate_grad)
    g_up = by_lang(feats, up_grad)
    g_down = by_lang(hidden, ups)
    squares = jnp.stack([
        jnp.sum(g_gate[l] ** 2, axis=0) + jnp.sum(g_up[l] ** 2, axis=0) + jnp.sum(g_down[l] ** 2, axis=1)
        for l in range(langs)
    ])
    moment = lax.psum(squares, "lang") / (3.0 * depth) + epsilon
    ratios = 1.0 / moment
    share = ratios / jnp.sum(ratios, axis=0, keepdims=True)

    def weigh(parts, axis):
        total = 0.0
        for l in range(langs):
            total = total + parts[l] * (share[l][None, :] if axis else share[l][:, None])
        return total.astype(jnp.bfloat16)

    return grad_tokens, weigh(g_gate, 1), weigh(g_up, 1), weigh(g_down, 0)


def solution(mesh):
    return jax.shard_map(
        functools.partial(body, mesh.shape["lang"], mesh.shape["fsdp"]),
        mesh=mesh,
        in_specs=(
            P("lang", "fsdp", None),
            P("lang", "fsdp", None),
            P("lang", None),
            P(None, "fsdp"),
            P(None, "fsdp"),
            P("fsdp", None),
        ),
        out_specs=(
            P("lang", "fsdp", None),
            P("lang", "fsdp"),
            P("lang", "fsdp"),
            P("fsdp", "lang"),
        ),
        check_vma=False,
    )
```
